256 devices in a mesh: morton: 32 (over x, y, core), coef: 8 (over z).
Axes of the slice: x: 4, y: 4, z: 8, core: 2. Of those that a mesh axis runs over, the one named last changes fastest.
Arguments:
- multipoles: bfloat16 [262144, 256], P(('morton', 'coef')), may hold values from -6 to 6
- send_rows: int32 [256, 32, 64], P(('morton', 'coef')), may hold values from 0 to 1023
- send_count: int32 [256, 32], P(('morton', 'coef')), may hold values from 0 to 64, as said below
- lists: int32 [262144, 32], P(('morton', 'coef')), may hold values from -1 to 4095, as said below
- operators: bfloat16 [32, 256, 256], replicated, may hold values from -0.0625 to 0.0625
- top_local: float32 [128, 256], P('morton'), may hold values from -6 to 6
- ancestor: int32 [262144], P(('morton', 'coef')), may hold values from 0 to 127
- down_ops: bfloat16 [8, 256, 256], replicated, may hold values from -0.375 to 0.375
Outputs:
- local_exp: float32 [262144, 256], P(('morton', 'coef'))
The draws below stay inside these ranges and needn't reach their ends.
Inputs may be any that keep to these rules, and one draw needn't show every extreme that they name: send_count of a sub-block to its own range is 0; to ranges within 2 of its own it is at most 64, and exactly 64 to the ranges one above and one below; to farther ranges at most 32, reached for the range 2 + 1 above. An entry of lists points into received only at slots below the matching send_count.
All inputs are finite; a program needn't handle non-finite values.
Results may differ from the reference program's by a relative error of at most 0.0022.
Values may be sent and summed in bfloat16 or wider, within the bound.
No kernel may reach another device: no remote copies, remote signals or barrier semaphores. Data moves between devices by JAX's collectives and lax.ppermute only.
A program may use at most 64 MiB of HBM per device.

```python
import jax
import jax.numpy as jnp
from jax import lax

COEFS = 256
SLOTS = 32
LEAF_DEV = 1024
SEND = 64
REACH = 2
RIM = 512
DEVS = 256
CELLS = 262144
TOP = 128
N_MORTON = 32
N_COEF = 8


def peer_counts(key):
    senders = jnp.arange(N_MORTON * N_COEF, dtype=jnp.int32)
    source_range = (senders // N_COEF)[:, None]
    target_range = jnp.arange(N_MORTON, dtype=jnp.int32)[None, :]
    distance = jnp.abs(source_range - target_range)
    grid = (N_MORTON * N_COEF, N_MORTON)
    near_draw = jax.random.randint(jax.random.fold_in(key, 101), grid, 3 * SEND // 4, SEND + 1)
    far_draw = jax.random.randint(jax.random.fold_in(key, 102), grid, 0, SEND // 2 + 1)
    counts = jnp.where(distance <= REACH, near_draw, far_draw)
    counts = jnp.where(distance == 1, SEND, counts)
    counts = jnp.where(target_range == source_range + REACH + 1, SEND // 2, counts)
    counts = jnp.where(distance == 0, 0, counts)
    return counts.astype(jnp.int32)


def draw_send_count(key, part):
    base = key
    return peer_counts(base)


def draw_lists(key, part):
    base = key
    key = jax.random.fold_in(key, 11)
    counts = peer_counts(base)
    keys = jax.random.split(key, 8)
    grid = (CELLS, SLOTS)
    rows = jnp.arange(CELLS, dtype=jnp.int32)[:, None]
    block = rows // LEAF_DEV
    range_index = block // N_COEF
    coef_index = block % N_COEF
    local_row = jax.random.randint(keys[0], grid, 0, LEAF_DEV + 2 * RIM)
    sign = 2 * jax.random.randint(keys[1], grid, 0, 2) - 1
    near_offset = jax.random.randint(keys[2], grid, 1, REACH + 1) * sign
    any_peer = jax.random.randint(keys[3], grid, 0, N_MORTON)
    use_near = jax.random.randint(keys[4], grid, 0, 2) == 1
    peer = jnp.where(use_near, range_index + near_offset, any_peer)
    slot = jax.random.randint(keys[5], grid, 0, SEND)
    inside = (peer >= 0) & (peer < N_MORTON) & (peer != range_index)
    peer_safe = jnp.clip(peer, 0, N_MORTON - 1)
    limit = counts[peer_safe * N_COEF + coef_index, range_index]
    attempt = jax.random.randint(keys[6], grid, 0, 5) < 2
    remote = inside & (slot < limit) & attempt
    entry = jnp.where(remote, LEAF_DEV + 2 * RIM + peer_safe * SEND + slot, local_row)
    empty = jax.random.randint(keys[7], grid, 0, 8) == 0
    return jnp.where(empty, -1, entry).astype(jnp.int32)


def touch_ends(values, key, least, high):
    index_at = [jax.random.randint(jax.random.fold_in(key, axis), (), 0, length) for axis, length in enumerate(values.shape)]
    main_axis = values.shape.index(max(values.shape))
    neighbour = index_at[:main_axis] + [(index_at[main_axis] + 1) % values.shape[main_axis]] + index_at[main_axis + 1:]
    return values.at[tuple(index_at)].set(least).at[tuple(neighbour)].set(high)


def steps_of(own_key, dims, cuts, smallest, largest):
    factor_of, own = 1.0, jax.random.fold_in(own_key, 6)
    for dim, blocks in cuts:
        heights = jnp.exp(jax.random.uniform(jax.random.fold_in(own, dim), (blocks,), jnp.float32, smallest / len(cuts), largest / len(cuts)))
        factor_of = factor_of * jnp.repeat(heights, dims[dim] // blocks).reshape([-1 if axis == dim else 1 for axis in range(len(dims))])
    return factor_of


def normal_values(key, shape, deviation, most, shards=(), kind=jnp.bfloat16):
    factor_of = steps_of(key, shape, shards, -0.22, 0.18) if shards else 1.0
    values = jax.random.normal(key, shape, jnp.float32) * deviation * factor_of
    return jnp.minimum(jnp.maximum(values, -most), most).astype(kind)


def setup_inputs(seed: int = 0) -> dict:
    arg_keys = jax.random.split(jax.random.key(seed), 9)
    multipoles = normal_values(arg_keys[0], (CELLS, COEFS), 1.0, 6.0, ((0, 256),))
    send_rows = touch_ends(jax.random.randint(arg_keys[1], (DEVS, N_MORTON, SEND), 0, LEAF_DEV), jax.random.fold_in(arg_keys[1], 1), 0, LEAF_DEV - 1).astype(jnp.int32)
    send_count = draw_send_count(jax.random.fold_in(arg_keys[8], 71), 0)
    lists = draw_lists(jax.random.fold_in(arg_keys[8], 71), 0)
    operators = normal_values(arg_keys[4], (SLOTS, COEFS, COEFS), (SLOTS * COEFS) ** -0.5, 0.0625)
    top_local = normal_values(arg_keys[5], (TOP, COEFS), 1.0, 6.0, ((0, 32),), jnp.float32)
    ancestor = touch_ends(jax.random.randint(arg_keys[6], (CELLS,), 0, TOP), jax.random.fold_in(arg_keys[6], 1), 0, TOP - 1).astype(jnp.int32)
    down_ops = normal_values(arg_keys[7], (8, COEFS, COEFS), COEFS ** -0.5, 0.375)
    return dict(multipoles=multipoles, send_rows=send_rows, send_count=send_count, lists=lists, operators=operators, top_local=top_local, ancestor=ancestor, down_ops=down_ops)


def reference(multipoles, send_rows, send_count, lists, operators, top_local, ancestor, down_ops):
    grouped = multipoles.reshape(N_MORTON, N_COEF, LEAF_DEV, COEFS)
    flat_ops = operators.astype(jnp.float32).reshape(SLOTS * COEFS, COEFS)
    down_wide = down_ops.astype(jnp.float32)
    peer_ids = jnp.arange(N_MORTON, dtype=jnp.int32)
    slot_ids = jnp.arange(SEND, dtype=jnp.int32)

    def per_block(block):
        range_index = block // N_COEF
        coef_index = block % N_COEF
        whole_range = grouped[range_index].reshape(N_COEF * LEAF_DEV, COEFS)
        padded = jnp.pad(whole_range, ((RIM, RIM), (0, 0)))
        nearby = lax.dynamic_slice_in_dim(padded, (coef_index * LEAF_DEV).astype(jnp.int32), LEAF_DEV + 2 * RIM, 0)
        senders = peer_ids * N_COEF + coef_index
        picked_rows = send_rows[senders, range_index]
        counts = send_count[senders, range_index]
        received = grouped[peer_ids[:, None], coef_index, picked_rows]
        keep = (slot_ids[None, :] < counts[:, None])[:, :, None]
        received = jnp.where(keep, received, jnp.zeros_like(received))
        table = jnp.concatenate([nearby, received.reshape(N_MORTON * SEND, COEFS)], 0)
        entries = lax.dynamic_slice_in_dim(lists, (block * LEAF_DEV).astype(jnp.int32), LEAF_DEV, 0)
        sources = table[jnp.maximum(entries, 0)]
        sources = jnp.where((entries >= 0)[:, :, None], sources, jnp.zeros_like(sources))
        far = jnp.dot(sources.reshape(LEAF_DEV, SLOTS * COEFS).astype(jnp.float32), flat_ops,
                      precision=lax.Precision.HIGHEST, preferred_element_type=jnp.float32)
        parents = lax.dynamic_slice_in_dim(ancestor, (block * LEAF_DEV).astype(jnp.int32), LEAF_DEV, 0)
        lifted = lax.optimization_barrier(top_local[parents].astype(jnp.bfloat16))
        lifted = lifted.astype(jnp.float32).reshape(LEAF_DEV // 8, 8, COEFS)
        inherited = jnp.einsum("nop,opq->noq", lifted, down_wide, precision=lax.Precision.HIGHEST)
        return far + inherited.reshape(LEAF_DEV, COEFS)

    return lax.map(per_block, jnp.arange(DEVS, dtype=jnp.int32)).reshape(CELLS, COEFS)
```

```python
import functools

import jax
import jax.numpy as jnp
from jax import lax
from jax.experimental import pallas as pl
from jax.experimental.pallas import tpu as pltpu
from jax.sharding import PartitionSpec as P

NEAR = (-2, -1, 1, 2)
SEND = 64
FAR_SLOTS = 32
LANES = 128
TARGETS = 256
CLASSES = 8
ROW_BLOCK = 32
WINDOW = 4096
BLANK = 2 * WINDOW
TOP_BASE = BLANK + 16


def send_kernel(peers, me_ref, pick_ref, cells_ref, top_ref, split_ref, out_ref, near_ref, table, rows):
    count = cells_ref.shape[0]
    step = 256
    for first in range(0, count, step):
        wide = cells_ref[first : first + step, :].astype(jnp.float32)
        table[pl.ds(2 * first, step, stride=2), :] = wide[:, :LANES]
        table[pl.ds(2 * first + 1, step, stride=2), :] = wide[:, LANES:]
    pitch = 2 * FAR_SLOTS + top_ref.shape[0]
    for peer in range(peers):
        for slot in range(FAR_SLOTS):
            source = pl.multiple_of(pick_ref[peer * SEND + slot], 2)
            rows[pl.ds(peer * pitch + 2 * slot, 2), :] = table[pl.ds(source, 2), :]
        rows[pl.ds(peer * pitch + 2 * FAR_SLOTS, top_ref.shape[0]), :] = top_ref[...]
        out_ref[peer] = rows[peer * pitch : (peer + 1) * pitch, :].astype(jnp.bfloat16)
    base = peers * pitch
    for near, distance in enumerate(NEAR):
        first = jnp.clip(me_ref[0] + distance, 0, peers - 1) * SEND + FAR_SLOTS
        for slot in range(FAR_SLOTS):
            source = pl.multiple_of(pick_ref[first + slot], 2)
            rows[pl.ds(base + 2 * slot, 2), :] = table[pl.ds(source, 2), :]
        near_ref[near] = rows[base : base + 2 * FAR_SLOTS, :].astype(jnp.bfloat16)
        base += 2 * FAR_SLOTS
    for first in range(0, 2 * count, 512):
        split_ref[first : first + 512, :] = table[first : first + 512, :].astype(jnp.bfloat16)


def main_kernel(
    peers,
    me_ref,
    index_ref,
    low_ref,
    own_ref,
    high_ref,
    incoming_ref,
    near_ref,
    ops_ref,
    down_ref,
    out_ref,
    table,
    index_a,
    index_b,
    index_top,
    picked_a,
    picked_b,
    total,
    index_sem,
):
    chunk = TARGETS * CLASSES
    slots = ops_ref.shape[0]
    groups = slots // CLASSES
    leaves = out_ref.shape[0]
    steps = leaves * slots // chunk
    indices = (index_a, index_b)
    picked = (picked_a, picked_b)

    def fetch(step, slot):
        first = pl.multiple_of(step * chunk, chunk)
        return pltpu.make_async_copy(
            index_ref.at[pl.ds(first, chunk)], indices[slot], index_sem.at[slot]
        )

    top_fetch = pltpu.make_async_copy(
        index_ref.at[pl.ds(leaves * slots, leaves)], index_top, index_sem.at[2]
    )
    top_fetch.start()
    fetch(0, 0).start()
    fetch(1, 1).start()

    def widen(source, rows, target):
        part = 512
        for first in range(0, rows, part):
            table[target + first : target + first + part, :] = source[
                first : first + part, :
            ].astype(jnp.float32)

    rim = low_ref.shape[0]
    own = own_ref.shape[0]
    widen(low_ref, rim, 0)
    widen(own_ref, own, rim)
    widen(high_ref, rim, rim + own)
    remote = 2 * rim + own
    per_peer = (BLANK - remote) // peers
    slab = 2 * FAR_SLOTS
    tops = incoming_ref.shape[1] - slab
    for peer in range(peers):
        part = incoming_ref[peer].astype(jnp.float32)
        table[remote + peer * per_peer : remote + peer * per_peer + slab, :] = part[:slab]
        table[TOP_BASE + peer * tops : TOP_BASE + (peer + 1) * tops, :] = part[slab:]
    table[BLANK:TOP_BASE, :] = jnp.zeros((TOP_BASE - BLANK, LANES), jnp.float32)
    for near, distance in enumerate(NEAR):
        peer = me_ref[0] - distance

        @pl.when((peer >= 0) & (peer < peers))
        def _():
            first = pl.multiple_of(remote + peer * per_peer + slab, slab)
            table[pl.ds(first, slab), :] = near_ref[near].astype(jnp.float32)

    def gather(where, position, target):
        source = pl.multiple_of(where[position], 2)
        target[pl.ds(2 * position, 2), :] = table[pl.ds(source, 2), :]

    def halves(rows, first, count):
        return [
            rows[pl.ds(2 * first + half, count, stride=2), :].astype(jnp.bfloat16)
            for half in range(2)
        ]

    top_fetch.wait()
    octants = down_ref.shape[0]
    share = leaves // octants
    for position in range(leaves):
        gather(index_top, position, picked_a)
    for octant in range(octants):
        lhs = jnp.concatenate(halves(picked_a, octant * share, share), axis=1)
        inherited = jnp.dot(lhs, down_ref[octant], preferred_element_type=jnp.float32)
        for half in range(2):
            total.at[half][pl.ds(octant, share, stride=octants), :] = inherited[
                :, half * LANES : (half + 1) * LANES
            ]

    def part_step(step, slot):
        fetch(step, slot).wait()
        for first in range(0, TARGETS, ROW_BLOCK):
            for member in range(CLASSES):
                for row in range(first, first + ROW_BLOCK):
                    gather(indices[slot], member * TARGETS + row, picked[slot])
        lhs = jnp.concatenate(
            [x for member in range(CLASSES) for x in halves(picked[slot], member * TARGETS, TARGETS)],
            axis=1,
        )
        group = step % groups
        rhs = ops_ref[pl.ds(group * CLASSES, CLASSES)].reshape(CLASSES * 2 * LANES, 2 * LANES)
        product = jnp.dot(lhs, rhs, preferred_element_type=jnp.float32)
        rows = pl.ds(pl.multiple_of(step // groups * TARGETS, TARGETS), TARGETS)
        for half in range(2):
            total[half, rows, :] += product[:, half * LANES : (half + 1) * LANES]

        @pl.when(step + 2 < steps)
        def _():
            fetch(step + 2, slot).start()

    def pair(index, carry):
        part_step(2 * index, 0)
        part_step(2 * index + 1, 1)
        return carry

    lax.fori_loop(0, steps // 2, pair, 0)
    for half in range(2):
        out_ref[:, half * LANES : (half + 1) * LANES] = total[half]


def on_device(multipoles, send_rows, send_count, lists, operators, top_local, ancestor, down_ops):
    leaves, coefs = multipoles.shape
    slots = operators.shape[0]
    peers = lax.axis_size("morton")
    me = lax.axis_index("morton")
    pick_rows = (2 * send_rows).reshape(-1)
    top_rows = top_local.reshape(-1, LANES)
    pitch = 2 * FAR_SLOTS + top_rows.shape[0]
    total_rows = peers * pitch + len(NEAR) * 2 * FAR_SLOTS
    vmem = pl.BlockSpec(memory_space=pltpu.VMEM)
    smem = pl.BlockSpec(memory_space=pltpu.SMEM)
    own, outgoing, near = pl.pallas_call(
        functools.partial(send_kernel, peers),
        out_shape=(
            jax.ShapeDtypeStruct((2 * leaves, LANES), jnp.bfloat16),
            jax.ShapeDtypeStruct((peers, pitch, LANES), jnp.bfloat16),
            jax.ShapeDtypeStruct((len(NEAR), 2 * FAR_SLOTS, LANES), jnp.bfloat16),
        ),
        in_specs=[smem, smem, vmem, vmem],
        out_specs=(vmem, vmem, vmem),
        scratch_shapes=[
            pltpu.VMEM((2 * leaves, LANES), jnp.float32),
            pltpu.VMEM((total_rows, LANES), jnp.float32),
        ],
        compiler_params=pltpu.CompilerParams(vmem_limit_bytes=16 * 2**20),
        name="send_rows",
    )(me[None], pick_rows, multipoles, top_rows)
    incoming = lax.all_to_all(outgoing, "morton", split_axis=0, concat_axis=0, tiled=True)
    ranks = lax.axis_size("coef")
    forward = [(i, i + 1) for i in range(ranks - 1)]
    backward = [(i + 1, i) for i in range(ranks - 1)]
    low = lax.ppermute(own[leaves:], "coef", forward)
    high = lax.ppermute(own[:leaves], "coef", backward)
    extras = [
        lax.ppermute(
            near[i],
            "morton",
            [(source, source + d) for source in range(peers) if 0 <= source + d < peers],
        )
        for i, d in enumerate(NEAR)
    ]
    near_in = jnp.stack(extras)
    entries = jnp.where(lists >= 0, 2 * lists, BLANK).T
    entries = entries.reshape(slots // CLASSES, CLASSES, leaves // TARGETS, TARGETS)
    entries = entries.transpose(2, 0, 1, 3).reshape(-1)
    octants = down_ops.shape[0]
    parents = (TOP_BASE + 2 * ancestor).reshape(leaves // octants, octants).T.reshape(-1)
    index = jnp.concatenate([entries, parents])
    chunk = TARGETS * CLASSES
    return pl.pallas_call(
        functools.partial(main_kernel, peers),
        out_shape=jax.ShapeDtypeStruct((leaves, coefs), jnp.float32),
        in_specs=[smem] + [vmem] * 8,
        out_specs=vmem,
        scratch_shapes=[
            pltpu.VMEM((TOP_BASE + peers * top_rows.shape[0], LANES), jnp.float32),
            pltpu.SMEM((chunk,), jnp.int32),
            pltpu.SMEM((chunk,), jnp.int32),
            pltpu.SMEM((leaves,), jnp.int32),
            pltpu.VMEM((2 * chunk, LANES), jnp.float32),
            pltpu.VMEM((2 * chunk, LANES), jnp.float32),
            pltpu.VMEM((2, leaves, LANES), jnp.float32),
            pltpu.SemaphoreType.DMA((3,)),
        ],
        compiler_params=pltpu.CompilerParams(vmem_limit_bytes=48 * 2**20),
        name="far_field",
    )(me[None], index, low, own, high, incoming, near_in, operators, down_ops)


def solution(mesh):
    placed = (
        P(("morton", "coef"), None),
        P(("morton", "coef"), None, None),
        P(("morton", "coef"), None),
        P(("morton", "coef"), None),
        P(),
        P("morton", None),
        P(("morton", "coef")),
        P(),
    )
    return jax.shard_map(
        on_device,
        mesh=mesh,
        in_specs=placed,
        out_specs=P(("morton", "coef"), None),
        check_vma=False,
    )
```

```python
import functools

import jax
import jax.numpy as jnp
from jax import lax
from jax.experimental import pallas as pl
from jax.experimental.pallas import tpu as pltpu
from jax.sharding import PartitionSpec as P

NEAR = (-2, -1, 1, 2)
FAR_SLOTS = 32
LANES = 128
TARGETS = 512
CLASSES = 16
SLOT_ROWS = 1024
WINDOW = 4096
BLANK = 2 * WINDOW
TOP_BASE = BLANK + 16


def split_rows(source, count, table, target, step=256):
    for first in range(0, count, step):
        wide = source[first : first + step, :].astype(jnp.float32)
        table[pl.ds(target + 2 * first, step, stride=2), :] = wide[:, :LANES]
        table[pl.ds(target + 2 * first + 1, step, stride=2), :] = wide[:, LANES:]


def send_kernel(
    peers, me_ref, pick_hbm, cells_hbm, top_hbm, out_ref, picks, cells, top, table, rows, sems
):
    copies = [
        pltpu.make_async_copy(source, target, sems.at[i])
        for i, (source, target) in enumerate(
            ((pick_hbm.at[0], picks), (cells_hbm, cells), (top_hbm, top))
        )
    ]
    for copy in copies:
        copy.start()
    tops = 2 * top.shape[0]
    slots = picks.shape[1]
    slab = 2 * slots
    pitch = slab + tops
    for first in range(0, rows.shape[0], pitch):
        rows[first : first + pitch, :] = jnp.zeros((pitch, LANES), jnp.float32)
    for copy in copies:
        copy.wait()
    split_rows(cells, cells.shape[0], table, 0)
    for half in range(2):
        part = top[:, half * LANES : (half + 1) * LANES]
        for peer in range(peers):
            rows[pl.ds(peer * pitch + slab + half, top.shape[0], stride=2), :] = part

    def pick(peer, slot, base):
        source = pl.multiple_of(2 * picks[peer, slot], 2)
        rows[pl.ds(pl.multiple_of(base + 2 * slot, 2), 2), :] = table[pl.ds(source, 2), :]

    for distance in NEAR:
        peer = jnp.clip(me_ref[0] + distance, 0, peers - 1)
        for slot in range(FAR_SLOTS, slots):
            pick(peer, slot, peer * pitch)
    for peer in range(peers):
        for slot in range(FAR_SLOTS):
            pick(peer, slot, peer * pitch)
        out_ref[peer] = rows[peer * pitch : (peer + 1) * pitch, :].astype(jnp.bfloat16)


def main_kernel(
    peers,
    index_ref,
    low_ref,
    own_ref,
    high_ref,
    incoming_ref,
    ops_ref,
    down_ref,
    out_ref,
    table,
    index_a,
    index_b,
    index_top,
    picked,
    total,
    index_sem,
):
    leaves = out_ref.shape[0]
    slots = ops_ref.shape[0]
    chunk = SLOT_ROWS
    per_block = TARGETS * slots // chunk
    steps = leaves * slots // chunk
    indices = (index_a, index_b)

    def fetch(step, slot):
        first = pl.multiple_of(step * chunk, chunk)
        return pltpu.make_async_copy(
            index_ref.at[pl.ds(first, chunk)], indices[slot], index_sem.at[slot]
        )

    top_fetch = pltpu.make_async_copy(
        index_ref.at[pl.ds(leaves * slots, leaves)], index_top, index_sem.at[2]
    )
    top_fetch.start()
    fetch(0, 0).start()
    fetch(1, 1).start()

    rim = 2 * low_ref.shape[0]
    own = 2 * own_ref.shape[0]
    split_rows(low_ref, low_ref.shape[0], table, 0)
    split_rows(own_ref, own_ref.shape[0], table, rim)
    split_rows(high_ref, high_ref.shape[0], table, rim + own)
    remote = 2 * rim + own
    per_peer = (BLANK - remote) // peers
    tops = incoming_ref.shape[1] - per_peer
    for peer in range(peers):
        part = incoming_ref[peer].astype(jnp.float32)
        table[remote + peer * per_peer : remote + (peer + 1) * per_peer, :] = part[:per_peer]
        table[TOP_BASE + peer * tops : TOP_BASE + (peer + 1) * tops, :] = part[per_peer:]
    table[BLANK:TOP_BASE, :] = jnp.zeros((TOP_BASE - BLANK, LANES), jnp.float32)
    def gather(where, position, base):
        source = pl.multiple_of(where[position], 2)
        target = pl.multiple_of(base + 2 * position, 2)
        picked[pl.ds(target, 2), :] = table[pl.ds(source, 2), :]

    def halves(rows, first, count):
        return [
            rows[pl.ds(2 * first + half, count, stride=2), :].astype(jnp.bfloat16)
            for half in range(2)
        ]

    top_fetch.wait()
    octants = down_ref.shape[0]
    share = leaves // octants
    for position in range(leaves):
        gather(index_top, position, 0)
    for octant in range(octants):
        lhs = jnp.concatenate(halves(picked, octant * share, share), axis=1)
        inherited = jnp.dot(lhs, down_ref[octant], preferred_element_type=jnp.float32)
        for half in range(2):
            total.at[half][pl.ds(octant, share, stride=octants), :] = inherited[
                :, half * LANES : (half + 1) * LANES
            ]

    def gather_step(step, base, slot):
        fetch(step, slot).wait()
        for row in range(chunk):
            gather(indices[slot], row, base)

        @pl.when(step + 2 < steps)
        def _():
            fetch(step + 2, slot).start()

    def block_step(block, carry):
        def pair(index, carry):
            base = pl.multiple_of(index * 4 * chunk, 4 * chunk)
            gather_step(block * per_block + 2 * index, base, 0)
            gather_step(block * per_block + 2 * index + 1, base + 2 * chunk, 1)
            return carry

        lax.fori_loop(0, per_block // 2, pair, 0)

        def multiply(group, carry):
            first = pl.multiple_of(group * CLASSES * TARGETS, CLASSES * TARGETS)
            lhs = jnp.concatenate(
                [
                    x
                    for member in range(CLASSES)
                    for x in halves(picked, first + member * TARGETS, TARGETS)
                ],
                axis=1,
            )
            rhs = ops_ref[pl.ds(group * CLASSES, CLASSES)]
            rhs = rhs.reshape(CLASSES * 2 * LANES, 2 * LANES)
            product = jnp.dot(lhs, rhs, preferred_element_type=jnp.float32)
            rows = pl.ds(pl.multiple_of(block * TARGETS, TARGETS), TARGETS)
            for half in range(2):
                total[half, rows, :] += product[:, half * LANES : (half + 1) * LANES]
            return carry

        lax.fori_loop(0, slots // CLASSES, multiply, 0)
        return carry

    lax.fori_loop(0, leaves // TARGETS, block_step, 0)
    for half in range(2):
        out_ref[:, half * LANES : (half + 1) * LANES] = total[half]


def on_device(multipoles, send_rows, send_count, lists, operators, top_local, ancestor, down_ops):
    leaves, coefs = multipoles.shape
    slots = operators.shape[0]
    peers = lax.axis_size("morton")
    me = lax.axis_index("morton")
    tops = 2 * top_local.shape[0]
    pitch = 2 * send_rows.shape[2] + tops
    total_rows = peers * pitch
    vmem = pl.BlockSpec(memory_space=pltpu.VMEM)
    smem = pl.BlockSpec(memory_space=pltpu.SMEM)
    hbm = pl.BlockSpec(memory_space=pltpu.HBM)
    outgoing = pl.pallas_call(
        functools.partial(send_kernel, peers),
        out_shape=jax.ShapeDtypeStruct((peers, pitch, LANES), jnp.bfloat16),
        in_specs=[smem, hbm, hbm, hbm],
        out_specs=vmem,
        scratch_shapes=[
            pltpu.SMEM(send_rows.shape[1:], jnp.int32),
            pltpu.VMEM(multipoles.shape, jnp.bfloat16),
            pltpu.VMEM(top_local.shape, jnp.float32),
            pltpu.VMEM((2 * leaves, LANES), jnp.float32),
            pltpu.VMEM((total_rows, LANES), jnp.float32),
            pltpu.SemaphoreType.DMA((3,)),
        ],
        compiler_params=pltpu.CompilerParams(vmem_limit_bytes=60 * 2**20),
        name="send_rows",
    )(me[None], send_rows, multipoles, top_local)
    incoming = lax.all_to_all(outgoing, "morton", split_axis=0, concat_axis=0, tiled=True)
    ranks = lax.axis_size("coef")
    forward = [(i, i + 1) for i in range(ranks - 1)]
    backward = [(i + 1, i) for i in range(ranks - 1)]
    low = lax.ppermute(multipoles[leaves // 2 :], "coef", forward)
    high = lax.ppermute(multipoles[: leaves // 2], "coef", backward)
    entries = jnp.where(lists >= 0, 2 * lists, BLANK).T
    entries = entries.reshape(slots, leaves // TARGETS, TARGETS).transpose(1, 0, 2).reshape(-1)
    octants = down_ops.shape[0]
    parents = (TOP_BASE + 2 * ancestor).reshape(leaves // octants, octants).T.reshape(-1)
    index = jnp.concatenate([entries, parents])
    chunk = SLOT_ROWS
    return pl.pallas_call(
        functools.partial(main_kernel, peers),
        out_shape=jax.ShapeDtypeStruct((leaves, coefs), jnp.float32),
        in_specs=[vmem] * 7,
        out_specs=vmem,
        scratch_shapes=[
            pltpu.VMEM((TOP_BASE + peers * tops, LANES), jnp.float32),
            pltpu.SMEM((chunk,), jnp.int32),
            pltpu.SMEM((chunk,), jnp.int32),
            pltpu.SMEM((leaves,), jnp.int32),
            pltpu.VMEM((2 * TARGETS * slots, LANES), jnp.float32),
            pltpu.VMEM((2, leaves, LANES), jnp.float32),
            pltpu.SemaphoreType.DMA((3,)),
        ],
        compiler_params=pltpu.CompilerParams(vmem_limit_bytes=48 * 2**20),
        name="far_field",
    )(index, low, multipoles, high, incoming, operators, down_ops)


def solution(mesh):
    placed = (
        P(("morton", "coef"), None),
        P(("morton", "coef"), None, None),
        P(("morton", "coef"), None),
        P(("morton", "coef"), None),
        P(),
        P("morton", None),
        P(("morton", "coef")),
        P(),
    )
    return jax.shard_map(
        on_device,
        mesh=mesh,
        in_specs=placed,
        out_specs=P(("morton", "coef"), None),
        check_vma=False,
    )
```

```python
import functools

import jax
import jax.numpy as jnp
from jax import lax
from jax.experimental import pallas as pl
from jax.experimental.pallas import tpu as pltpu
from jax.sharding import PartitionSpec as P

NEAR = (-2, -1, 1, 2)
FAR_SLOTS = 32
LANES = 128
TARGETS = 512
CLASSES = 32
SLOT_ROWS = 1024
WINDOW = 4096
BLANK = 2 * WINDOW


def split_rows(source, count, table, target, step=256):
    for first in range(0, count, step):
        wide = source[first : first + step, :].astype(jnp.float32)
        table[pl.ds(target + 2 * first, step, stride=2), :] = wide[:, :LANES]
        table[pl.ds(target + 2 * first + 1, step, stride=2), :] = wide[:, LANES:]


def send_kernel(
    peers, me_ref, pick_hbm, cells_hbm, top_hbm, out_ref, picks, cells, top, table, rows, sems
):
    copies = [
        pltpu.make_async_copy(source, target, sems.at[i])
        for i, (source, target) in enumerate(
            ((pick_hbm.at[0], picks), (cells_hbm, cells), (top_hbm, top))
        )
    ]
    for copy in copies:
        copy.start()
    tops = 2 * top.shape[0]
    slots = picks.shape[1]
    slab = 2 * slots
    pitch = slab + tops
    for first in range(0, rows.shape[0], pitch):
        rows[first : first + pitch, :] = jnp.zeros((pitch, LANES), jnp.float32)
    copies[0].wait()
    copies[1].wait()
    split_rows(cells, cells.shape[0], table, 0)
    copies[2].wait()
    for half in range(2):
        part = top[:, half * LANES : (half + 1) * LANES]
        for peer in range(peers):
            rows[pl.ds(peer * pitch + slab + half, top.shape[0], stride=2), :] = part


    def pick(peer, slot, base):
        source = pl.multiple_of(2 * picks[peer, slot], 2)
        rows[pl.ds(pl.multiple_of(base + 2 * slot, 2), 2), :] = table[pl.ds(source, 2), :]

    for distance in NEAR:
        peer = jnp.clip(me_ref[0] + distance, 0, peers - 1)
        for slot in range(FAR_SLOTS, slots):
            pick(peer, slot, peer * pitch)
    for peer in range(peers):
        for slot in range(FAR_SLOTS):
            pick(peer, slot, peer * pitch)
        out_ref[peer] = rows[peer * pitch : (peer + 1) * pitch, :].astype(jnp.bfloat16)


def main_kernel(
    peers,
    index_ref,
    parent_ref,
    low_ref,
    own_ref,
    high_ref,
    incoming_ref,
    ops_hbm,
    down_hbm,
    out_hbm,
    table,
    index_a,
    index_b,
    top_table,
    picked,
    total,
    ops_ref,
    down_ref,
    staged,
    index_sem,
    weight_sem,
    out_sem,
):
    leaves = out_hbm.shape[0]
    slots = ops_ref.shape[0]
    chunk = SLOT_ROWS
    per_block = TARGETS * slots // chunk
    steps = leaves * slots // chunk
    indices = (index_a, index_b)

    def fetch(step, slot):
        first = pl.multiple_of(step * chunk, chunk)
        return pltpu.make_async_copy(
            index_ref.at[pl.ds(first, chunk)], indices[slot], index_sem.at[slot]
        )

    weights = [
        pltpu.make_async_copy(source, target, weight_sem.at[i])
        for i, (source, target) in enumerate(((down_hbm, down_ref), (ops_hbm, ops_ref)))
    ]
    fetch(0, 0).start()
    fetch(1, 1).start()
    for weight in weights:
        weight.start()

    rim = 2 * low_ref.shape[0]
    own = 2 * own_ref.shape[0]
    split_rows(low_ref, low_ref.shape[0], table, 0)
    split_rows(own_ref, own_ref.shape[0], table, rim)
    split_rows(high_ref, high_ref.shape[0], table, rim + own)
    remote = 2 * rim + own
    per_peer = (BLANK - remote) // peers
    tops = incoming_ref.shape[1] - per_peer
    for peer in range(peers):
        part = incoming_ref[peer].astype(jnp.float32)
        table[remote + peer * per_peer : remote + (peer + 1) * per_peer, :] = part[:per_peer]
        top_table[peer * tops : (peer + 1) * tops, :] = part[per_peer:]
    table[BLANK:, :] = jnp.zeros((table.shape[0] - BLANK, LANES), jnp.float32)
    def gather(where, position, base):
        source = pl.multiple_of(where[position], 2)
        target = pl.multiple_of(base + 2 * position, 2)
        picked[pl.ds(target, 2), :] = table[pl.ds(source, 2), :]

    def halves(rows, first, count):
        return [
            rows[pl.ds(2 * first + half, count, stride=2), :].astype(jnp.bfloat16)
            for half in range(2)
        ]

    weights[0].wait()
    octants = down_ref.shape[0]
    share = leaves // octants
    top_count = top_table.shape[0] // 2
    top_rows = jnp.concatenate(
        [
            top_table[pl.ds(half, top_count, stride=2), :].astype(jnp.bfloat16)
            for half in range(2)
        ],
        axis=1,
    )
    top_ids = lax.broadcasted_iota(jnp.int32, (top_count, share), 0)
    for octant in range(octants):
        chosen = jnp.where(top_ids == parent_ref[octant : octant + 1, :], 1.0, 0.0)
        lifted = lax.dot_general(
            chosen.astype(jnp.bfloat16),
            top_rows,
            (((0,), (0,)), ((), ())),
            preferred_element_type=jnp.float32,
        ).astype(jnp.bfloat16)
        inherited = jnp.dot(lifted, down_ref[octant], preferred_element_type=jnp.float32)
        for half in range(2):
            total.at[half][pl.ds(octant, share, stride=octants), :] = inherited[
                :, half * LANES : (half + 1) * LANES
            ]

    def gather_step(step, base, slot):
        fetch(step, slot).wait()
        for row in range(chunk):
            gather(indices[slot], row, base)

        @pl.when(step + 2 < steps)
        def _():
            fetch(step + 2, slot).start()

    def send_out(block):
        rows = pl.ds(pl.multiple_of(block * TARGETS, TARGETS), TARGETS)
        return pltpu.make_async_copy(staged.at[rows], out_hbm.at[rows], out_sem.at[block])

    def block_step(block, carry):
        def pair(index, carry):
            base = pl.multiple_of(index * 4 * chunk, 4 * chunk)
            gather_step(block * per_block + 2 * index, base, 0)
            gather_step(block * per_block + 2 * index + 1, base + 2 * chunk, 1)
            return carry

        lax.fori_loop(0, per_block // 2, pair, 0)

        @pl.when(block == 0)
        def _():
            weights[1].wait()

        def multiply(group, carry):
            first = pl.multiple_of(group * CLASSES * TARGETS, CLASSES * TARGETS)
            lhs = jnp.concatenate(
                [
                    x
                    for member in range(CLASSES)
                    for x in halves(picked, first + member * TARGETS, TARGETS)
                ],
                axis=1,
            )
            rhs = ops_ref[pl.ds(group * CLASSES, CLASSES)]
            rhs = rhs.reshape(CLASSES * 2 * LANES, 2 * LANES)
            product = jnp.dot(lhs, rhs, preferred_element_type=jnp.float32)
            rows = pl.ds(pl.multiple_of(block * TARGETS, TARGETS), TARGETS)
            for half in range(2):
                total[half, rows, :] += product[:, half * LANES : (half + 1) * LANES]
            return carry

        lax.fori_loop(0, slots // CLASSES, multiply, 0)
        rows = pl.ds(pl.multiple_of(block * TARGETS, TARGETS), TARGETS)
        for half in range(2):
            staged[rows, half * LANES : (half + 1) * LANES] = total[half, rows, :]
        send_out(block).start()
        return carry

    lax.fori_loop(0, leaves // TARGETS, block_step, 0)
    for block in range(leaves // TARGETS):
        send_out(block).wait()


def on_device(multipoles, send_rows, send_count, lists, operators, top_local, ancestor, down_ops):
    leaves, coefs = multipoles.shape
    slots = operators.shape[0]
    peers = lax.axis_size("morton")
    me = lax.axis_index("morton")
    tops = 2 * top_local.shape[0]
    pitch = 2 * send_rows.shape[2] + tops
    total_rows = peers * pitch
    vmem = pl.BlockSpec(memory_space=pltpu.VMEM)
    smem = pl.BlockSpec(memory_space=pltpu.SMEM)
    hbm = pl.BlockSpec(memory_space=pltpu.HBM)
    outgoing = pl.pallas_call(
        functools.partial(send_kernel, peers),
        out_shape=jax.ShapeDtypeStruct((peers, pitch, LANES), jnp.bfloat16),
        in_specs=[smem, hbm, hbm, hbm],
        out_specs=vmem,
        scratch_shapes=[
            pltpu.SMEM(send_rows.shape[1:], jnp.int32),
            pltpu.VMEM(multipoles.shape, jnp.bfloat16),
            pltpu.VMEM(top_local.shape, jnp.float32),
            pltpu.VMEM((2 * leaves, LANES), jnp.float32),
            pltpu.VMEM((total_rows, LANES), jnp.float32),
            pltpu.SemaphoreType.DMA((3,)),
        ],
        compiler_params=pltpu.CompilerParams(vmem_limit_bytes=60 * 2**20),
        name="send_rows",
    )(me[None], send_rows, multipoles, top_local)
    incoming = lax.all_to_all(outgoing, "morton", split_axis=0, concat_axis=0, tiled=True)
    ranks = lax.axis_size("coef")
    forward = [(i, i + 1) for i in range(ranks - 1)]
    backward = [(i + 1, i) for i in range(ranks - 1)]
    low = lax.ppermute(multipoles[leaves // 2 :], "coef", forward)
    high = lax.ppermute(multipoles[: leaves // 2], "coef", backward)
    entries = jnp.where(lists >= 0, 2 * lists, BLANK).T
    entries = entries.reshape(slots, leaves // TARGETS, TARGETS).transpose(1, 0, 2).reshape(-1)
    octants = down_ops.shape[0]
    parents = ancestor.reshape(leaves // octants, octants).T
    chunk = SLOT_ROWS
    return pl.pallas_call(
        functools.partial(main_kernel, peers),
        out_shape=jax.ShapeDtypeStruct((leaves, coefs), jnp.float32),
        in_specs=[vmem] * 6 + [hbm] * 2,
        out_specs=hbm,
        scratch_shapes=[
            pltpu.VMEM((BLANK + 16, LANES), jnp.float32),
            pltpu.SMEM((chunk,), jnp.int32),
            pltpu.SMEM((chunk,), jnp.int32),
            pltpu.VMEM((peers * tops, LANES), jnp.float32),
            pltpu.VMEM((2 * TARGETS * slots, LANES), jnp.float32),
            pltpu.VMEM((2, leaves, LANES), jnp.float32),
            pltpu.VMEM(operators.shape, operators.dtype),
            pltpu.VMEM(down_ops.shape, down_ops.dtype),
            pltpu.VMEM((leaves, coefs), jnp.float32),
            pltpu.SemaphoreType.DMA((2,)),
            pltpu.SemaphoreType.DMA((2,)),
            pltpu.SemaphoreType.DMA((leaves // TARGETS,)),
        ],
        compiler_params=pltpu.CompilerParams(vmem_limit_bytes=48 * 2**20),
        name="far_field",
    )(entries, parents, low, multipoles, high, incoming, operators, down_ops)


def solution(mesh):
    placed = (
        P(("morton", "coef"), None),
        P(("morton", "coef"), None, None),
        P(("morton", "coef"), None),
        P(("morton", "coef"), None),
        P(),
        P("morton", None),
        P(("morton", "coef")),
        P(),
    )
    return jax.shard_map(
        on_device,
        mesh=mesh,
        in_specs=placed,
        out_specs=P(("morton", "coef"), None),
        check_vma=False,
    )
```

```python
import functools

import jax
import jax.numpy as jnp
from jax import lax
from jax.experimental import pallas as pl
from jax.experimental.pallas import tpu as pltpu
from jax.sharding import PartitionSpec as P

NEAR = (-2, -1, 1, 2)
FAR_SLOTS = 32
PEER_GROUP = 8
LANES = 128
TARGETS = 512
CLASSES = 32
SLOT_ROWS = 1024
WINDOW = 4096
BLANK = 2 * WINDOW


def split_rows(source, count, table, target, step=256):
    for first in range(0, count, step):
        wide = source[first : first + step, :].astype(jnp.float32)
        table[pl.ds(target + 2 * first, step, stride=2), :] = wide[:, :LANES]
        table[pl.ds(target + 2 * first + 1, step, stride=2), :] = wide[:, LANES:]


def send_kernel(
    peers, me_ref, pick_hbm, cells_hbm, top_hbm, out_hbm, picks, cells, top, table, rows, packed, sems, out_sems
):
    copies = [
        pltpu.make_async_copy(source, target, sems.at[i])
        for i, (source, target) in enumerate(
            ((pick_hbm.at[0], picks), (cells_hbm, cells), (top_hbm, top))
        )
    ]
    for copy in copies:
        copy.start()
    tops = 2 * top.shape[0]
    slots = picks.shape[1]
    slab = 2 * slots
    pitch = slab + tops
    for first in range(0, rows.shape[0], pitch):
        rows[first : first + pitch, :] = jnp.zeros((pitch, LANES), jnp.float32)
    copies[0].wait()
    copies[1].wait()
    split_rows(cells, cells.shape[0], table, 0)
    copies[2].wait()
    for half in range(2):
        part = top[:, half * LANES : (half + 1) * LANES]
        for peer in range(peers):
            rows[pl.ds(peer * pitch + slab + half, top.shape[0], stride=2), :] = part


    def send_group(group):
        part = pl.ds(group * PEER_GROUP, PEER_GROUP)
        return pltpu.make_async_copy(packed.at[part], out_hbm.at[part], out_sems.at[group])

    def pick(peer, slot, base):
        source = pl.multiple_of(2 * picks[peer, slot], 2)
        rows[pl.ds(pl.multiple_of(base + 2 * slot, 2), 2), :] = table[pl.ds(source, 2), :]

    for distance in NEAR:
        peer = jnp.clip(me_ref[0] + distance, 0, peers - 1)
        for slot in range(FAR_SLOTS, slots):
            pick(peer, slot, peer * pitch)
    for peer in range(peers):
        for slot in range(FAR_SLOTS):
            pick(peer, slot, peer * pitch)
        packed[peer] = rows[peer * pitch : (peer + 1) * pitch, :].astype(jnp.bfloat16)
        if peer % PEER_GROUP == PEER_GROUP - 1:
            send_group(peer // PEER_GROUP).start()
    for group in range(peers // PEER_GROUP):
        send_group(group).wait()


def main_kernel(
    peers,
    index_ref,
    parent_ref,
    low_ref,
    own_ref,
    high_ref,
    incoming_ref,
    ops_hbm,
    down_hbm,
    out_hbm,
    table,
    index_a,
    index_b,
    top_table,
    picked,
    total,
    ops_ref,
    down_ref,
    staged,
    index_sem,
    weight_sem,
    out_sem,
):
    leaves = out_hbm.shape[0]
    slots = ops_ref.shape[0]
    chunk = SLOT_ROWS
    per_block = TARGETS * slots // chunk
    steps = leaves * slots // chunk
    indices = (index_a, index_b)

    def fetch(step, slot):
        first = pl.multiple_of(step * chunk, chunk)
        return pltpu.make_async_copy(
            index_ref.at[pl.ds(first, chunk)], indices[slot], index_sem.at[slot]
        )

    weights = [
        pltpu.make_async_copy(source, target, weight_sem.at[i])
        for i, (source, target) in enumerate(((down_hbm, down_ref), (ops_hbm, ops_ref)))
    ]
    fetch(0, 0).start()
    fetch(1, 1).start()
    for weight in weights:
        weight.start()

    rim = 2 * low_ref.shape[0]
    own = 2 * own_ref.shape[0]
    split_rows(low_ref, low_ref.shape[0], table, 0)
    split_rows(own_ref, own_ref.shape[0], table, rim)
    split_rows(high_ref, high_ref.shape[0], table, rim + own)
    remote = 2 * rim + own
    per_peer = (BLANK - remote) // peers
    tops = incoming_ref.shape[1] - per_peer
    for peer in range(peers):
        part = incoming_ref[peer].astype(jnp.float32)
        table[remote + peer * per_peer : remote + (peer + 1) * per_peer, :] = part[:per_peer]
        top_table[peer * tops : (peer + 1) * tops, :] = part[per_peer:]
    table[BLANK:, :] = jnp.zeros((table.shape[0] - BLANK, LANES), jnp.float32)
    def gather(where, position, base):
        source = pl.multiple_of(where[position], 2)
        target = pl.multiple_of(base + 2 * position, 2)
        picked[pl.ds(target, 2), :] = table[pl.ds(source, 2), :]

    def halves(rows, first, count):
        return [
            rows[pl.ds(2 * first + half, count, stride=2), :].astype(jnp.bfloat16)
            for half in range(2)
        ]

    weights[0].wait()
    octants = down_ref.shape[0]
    share = leaves // octants
    top_count = top_table.shape[0] // 2
    top_rows = jnp.concatenate(
        [
            top_table[pl.ds(half, top_count, stride=2), :].astype(jnp.bfloat16)
            for half in range(2)
        ],
        axis=1,
    )
    top_ids = lax.broadcasted_iota(jnp.int32, (top_count, share), 0)
    for octant in range(octants):
        chosen = jnp.where(top_ids == parent_ref[octant : octant + 1, :], 1.0, 0.0)
        lifted = lax.dot_general(
            chosen.astype(jnp.bfloat16),
            top_rows,
            (((0,), (0,)), ((), ())),
            preferred_element_type=jnp.float32,
        ).astype(jnp.bfloat16)
        inherited = jnp.dot(lifted, down_ref[octant], preferred_element_type=jnp.float32)
        for half in range(2):
            total.at[half][pl.ds(octant, share, stride=octants), :] = inherited[
                :, half * LANES : (half + 1) * LANES
            ]

    def gather_step(step, base, slot):
        fetch(step, slot).wait()
        for row in range(chunk):
            gather(indices[slot], row, base)

        @pl.when(step + 2 < steps)
        def _():
            fetch(step + 2, slot).start()

    def send_out(block):
        rows = pl.ds(pl.multiple_of(block * TARGETS, TARGETS), TARGETS)
        return pltpu.make_async_copy(staged.at[rows], out_hbm.at[rows], out_sem.at[block])

    def block_step(block, carry):
        def pair(index, carry):
            base = pl.multiple_of(index * 4 * chunk, 4 * chunk)
            gather_step(block * per_block + 2 * index, base, 0)
            gather_step(block * per_block + 2 * index + 1, base + 2 * chunk, 1)
            return carry

        lax.fori_loop(0, per_block // 2, pair, 0)

        @pl.when(block == 0)
        def _():
            weights[1].wait()

        def multiply(group, carry):
            first = pl.multiple_of(group * CLASSES * TARGETS, CLASSES * TARGETS)
            lhs = jnp.concatenate(
                [
                    x
                    for member in range(CLASSES)
                    for x in halves(picked, first + member * TARGETS, TARGETS)
                ],
                axis=1,
            )
            rhs = ops_ref[pl.ds(group * CLASSES, CLASSES)]
            rhs = rhs.reshape(CLASSES * 2 * LANES, 2 * LANES)
            product = jnp.dot(lhs, rhs, preferred_element_type=jnp.float32)
            rows = pl.ds(pl.multiple_of(block * TARGETS, TARGETS), TARGETS)
            for half in range(2):
                total[half, rows, :] += product[:, half * LANES : (half + 1) * LANES]
            return carry

        lax.fori_loop(0, slots // CLASSES, multiply, 0)
        rows = pl.ds(pl.multiple_of(block * TARGETS, TARGETS), TARGETS)
        for half in range(2):
            staged[rows, half * LANES : (half + 1) * LANES] = total[half, rows, :]
        send_out(block).start()
        return carry

    lax.fori_loop(0, leaves // TARGETS, block_step, 0)
    for block in range(leaves // TARGETS):
        send_out(block).wait()


def on_device(multipoles, send_rows, send_count, lists, operators, top_local, ancestor, down_ops):
    leaves, coefs = multipoles.shape
    slots = operators.shape[0]
    peers = lax.axis_size("morton")
    me = lax.axis_index("morton")
    tops = 2 * top_local.shape[0]
    pitch = 2 * send_rows.shape[2] + tops
    total_rows = peers * pitch
    vmem = pl.BlockSpec(memory_space=pltpu.VMEM)
    smem = pl.BlockSpec(memory_space=pltpu.SMEM)
    hbm = pl.BlockSpec(memory_space=pltpu.HBM)
    outgoing = pl.pallas_call(
        functools.partial(send_kernel, peers),
        out_shape=jax.ShapeDtypeStruct((peers, pitch, LANES), jnp.bfloat16),
        in_specs=[smem, hbm, hbm, hbm],
        out_specs=hbm,
        scratch_shapes=[
            pltpu.SMEM(send_rows.shape[1:], jnp.int32),
            pltpu.VMEM(multipoles.shape, jnp.bfloat16),
            pltpu.VMEM(top_local.shape, jnp.float32),
            pltpu.VMEM((2 * leaves, LANES), jnp.float32),
            pltpu.VMEM((total_rows, LANES), jnp.float32),
            pltpu.VMEM((peers, pitch, LANES), jnp.bfloat16),
            pltpu.SemaphoreType.DMA((3,)),
            pltpu.SemaphoreType.DMA((peers // PEER_GROUP,)),
        ],
        compiler_params=pltpu.CompilerParams(vmem_limit_bytes=60 * 2**20),
        name="send_rows",
    )(me[None], send_rows, multipoles, top_local)
    incoming = lax.all_to_all(outgoing, "morton", split_axis=0, concat_axis=0, tiled=True)
    ranks = lax.axis_size("coef")
    forward = [(i, i + 1) for i in range(ranks - 1)]
    backward = [(i + 1, i) for i in range(ranks - 1)]
    low = lax.ppermute(multipoles[leaves // 2 :], "coef", forward)
    high = lax.ppermute(multipoles[: leaves // 2], "coef", backward)
    entries = jnp.where(lists >= 0, 2 * lists, BLANK).T
    entries = entries.reshape(slots, leaves // TARGETS, TARGETS).transpose(1, 0, 2).reshape(-1)
    octants = down_ops.shape[0]
    parents = ancestor.reshape(leaves // octants, octants).T
    chunk = SLOT_ROWS
    return pl.pallas_call(
        functools.partial(main_kernel, peers),
        out_shape=jax.ShapeDtypeStruct((leaves, coefs), jnp.float32),
        in_specs=[vmem] * 6 + [hbm] * 2,
        out_specs=hbm,
        scratch_shapes=[
            pltpu.VMEM((BLANK + 16, LANES), jnp.float32),
            pltpu.SMEM((chunk,), jnp.int32),
            pltpu.SMEM((chunk,), jnp.int32),
            pltpu.VMEM((peers * tops, LANES), jnp.float32),
            pltpu.VMEM((2 * TARGETS * slots, LANES), jnp.float32),
            pltpu.VMEM((2, leaves, LANES), jnp.float32),
            pltpu.VMEM(operators.shape, operators.dtype),
            pltpu.VMEM(down_ops.shape, down_ops.dtype),
            pltpu.VMEM((leaves, coefs), jnp.float32),
            pltpu.SemaphoreType.DMA((2,)),
            pltpu.SemaphoreType.DMA((2,)),
            pltpu.SemaphoreType.DMA((leaves // TARGETS,)),
        ],
        compiler_params=pltpu.CompilerParams(vmem_limit_bytes=48 * 2**20),
        name="far_field",
    )(entries, parents, low, multipoles, high, incoming, operators, down_ops)


def solution(mesh):
    placed = (
        P(("morton", "coef"), None),
        P(("morton", "coef"), None, None),
        P(("morton", "coef"), None),
        P(("morton", "coef"), None),
        P(),
        P("morton", None),
        P(("morton", "coef")),
        P(),
    )
    return jax.shard_map(
        on_device,
        mesh=mesh,
        in_specs=placed,
        out_specs=P(("morton", "coef"), None),
        check_vma=False,
    )
```

```python
import functools

import jax
import jax.numpy as jnp
from jax import lax
from jax.experimental import pallas as pl
from jax.experimental.pallas import tpu as pltpu
from jax.sharding import PartitionSpec as P

NEAR = (-2, -1, 1, 2)
FAR_SLOTS = 32
PEER_GROUP = 8
LANES = 128
TARGETS = 512
CLASSES = 32
SLOT_ROWS = 2048
WINDOW = 4096
BLANK = 2 * WINDOW


def split_rows(source, count, table, target, step=256):
    for first in range(0, count, step):
        wide = source[first : first + step, :].astype(jnp.float32)
        table[pl.ds(target + 2 * first, step, stride=2), :] = wide[:, :LANES]
        table[pl.ds(target + 2 * first + 1, step, stride=2), :] = wide[:, LANES:]


def send_kernel(
    peers, me_ref, pick_hbm, cells_hbm, top_hbm, out_hbm, picks, cells, top, table, rows, packed, sems, out_sems
):
    copies = [
        pltpu.make_async_copy(source, target, sems.at[i])
        for i, (source, target) in enumerate(
            ((pick_hbm.at[0], picks), (top_hbm, top))
        )
    ]
    quarter = cells.shape[0] // 4
    for i in range(4):
        part = pl.ds(i * quarter, quarter)
        copies.append(pltpu.make_async_copy(cells_hbm.at[part], cells.at[part], sems.at[2 + i]))
    for copy in copies:
        copy.start()
    tops = 2 * top.shape[0]
    slots = picks.shape[1]
    slab = 2 * slots
    pitch = slab + tops
    for first in range(0, rows.shape[0], pitch):
        rows[first : first + pitch, :] = jnp.zeros((pitch, LANES), jnp.float32)
    for i in range(4):
        copies[2 + i].wait()
        part = cells.at[pl.ds(i * quarter, quarter)]
        split_rows(part, quarter, table, 2 * i * quarter)
    copies[0].wait()
    copies[1].wait()
    for half in range(2):
        part = top[:, half * LANES : (half + 1) * LANES]
        for peer in range(peers):
            rows[pl.ds(peer * pitch + slab + half, top.shape[0], stride=2), :] = part


    def send_group(group):
        part = pl.ds(group * PEER_GROUP, PEER_GROUP)
        return pltpu.make_async_copy(packed.at[part], out_hbm.at[part], out_sems.at[group])

    def pick(peer, slot, base):
        source = pl.multiple_of(2 * picks[peer, slot], 2)
        rows[pl.ds(pl.multiple_of(base + 2 * slot, 2), 2), :] = table[pl.ds(source, 2), :]

    for distance in NEAR:
        peer = jnp.clip(me_ref[0] + distance, 0, peers - 1)
        for slot in range(FAR_SLOTS, slots):
            pick(peer, slot, peer * pitch)
    for peer in range(peers):
        for slot in range(FAR_SLOTS):
            pick(peer, slot, peer * pitch)
        packed[peer] = rows[peer * pitch : (peer + 1) * pitch, :].astype(jnp.bfloat16)
        if peer % PEER_GROUP == PEER_GROUP - 1:
            send_group(peer // PEER_GROUP).start()
    for group in range(peers // PEER_GROUP):
        send_group(group).wait()


def main_kernel(
    peers,
    index_ref,
    parent_ref,
    low_ref,
    own_ref,
    high_ref,
    incoming_ref,
    ops_hbm,
    down_hbm,
    out_hbm,
    table,
    index_a,
    index_b,
    top_table,
    picked,
    total,
    ops_ref,
    down_ref,
    staged,
    index_sem,
    weight_sem,
    out_sem,
):
    leaves = out_hbm.shape[0]
    slots = ops_ref.shape[0]
    chunk = SLOT_ROWS
    per_block = TARGETS * slots // chunk
    steps = leaves * slots // chunk
    indices = (index_a, index_b)

    def fetch(step, slot):
        first = pl.multiple_of(step * chunk, chunk)
        return pltpu.make_async_copy(
            index_ref.at[pl.ds(first, chunk)], indices[slot], index_sem.at[slot]
        )

    weights = [
        pltpu.make_async_copy(source, target, weight_sem.at[i])
        for i, (source, target) in enumerate(((down_hbm, down_ref), (ops_hbm, ops_ref)))
    ]
    fetch(0, 0).start()
    fetch(1, 1).start()
    for weight in weights:
        weight.start()

    rim = 2 * low_ref.shape[0]
    own = 2 * own_ref.shape[0]
    split_rows(low_ref, low_ref.shape[0], table, 0)
    split_rows(own_ref, own_ref.shape[0], table, rim)
    split_rows(high_ref, high_ref.shape[0], table, rim + own)
    remote = 2 * rim + own
    per_peer = (BLANK - remote) // peers
    tops = incoming_ref.shape[1] - per_peer
    for peer in range(peers):
        part = incoming_ref[peer].astype(jnp.float32)
        table[remote + peer * per_peer : remote + (peer + 1) * per_peer, :] = part[:per_peer]
        top_table[peer * tops : (peer + 1) * tops, :] = part[per_peer:]
    table[BLANK:, :] = jnp.zeros((table.shape[0] - BLANK, LANES), jnp.float32)
    def gather(where, position, base):
        source = pl.multiple_of(where[position], 2)
        target = pl.multiple_of(base + 2 * position, 2)
        picked[pl.ds(target, 2), :] = table[pl.ds(source, 2), :]

    def halves(rows, first, count):
        return [
            rows[pl.ds(2 * first + half, count, stride=2), :].astype(jnp.bfloat16)
            for half in range(2)
        ]

    weights[0].wait()
    octants = down_ref.shape[0]
    share = leaves // octants
    top_count = top_table.shape[0] // 2
    top_rows = jnp.concatenate(
        [
            top_table[pl.ds(half, top_count, stride=2), :].astype(jnp.bfloat16)
            for half in range(2)
        ],
        axis=1,
    )
    top_ids = lax.broadcasted_iota(jnp.int32, (top_count, share), 0)
    for octant in range(octants):
        chosen = jnp.where(top_ids == parent_ref[octant : octant + 1, :], 1.0, 0.0)
        lifted = lax.dot_general(
            chosen.astype(jnp.bfloat16),
            top_rows,
            (((0,), (0,)), ((), ())),
            preferred_element_type=jnp.float32,
        ).astype(jnp.bfloat16)
        inherited = jnp.dot(lifted, down_ref[octant], preferred_element_type=jnp.float32)
        for half in range(2):
            total.at[half][pl.ds(octant, share, stride=octants), :] = inherited[
                :, half * LANES : (half + 1) * LANES
            ]

    def gather_step(step, base, slot):
        fetch(step, slot).wait()
        for row in range(chunk):
            gather(indices[slot], row, base)

        @pl.when(step + 2 < steps)
        def _():
            fetch(step + 2, slot).start()

    def send_out(block):
        rows = pl.ds(pl.multiple_of(block * TARGETS, TARGETS), TARGETS)
        return pltpu.make_async_copy(staged.at[rows], out_hbm.at[rows], out_sem.at[block])

    def block_step(block, carry):
        def pair(index, carry):
            base = pl.multiple_of(index * 4 * chunk, 4 * chunk)
            gather_step(block * per_block + 2 * index, base, 0)
            gather_step(block * per_block + 2 * index + 1, base + 2 * chunk, 1)
            return carry

        lax.fori_loop(0, per_block // 2, pair, 0)

        @pl.when(block == 0)
        def _():
            weights[1].wait()

        def multiply(group, carry):
            first = pl.multiple_of(group * CLASSES * TARGETS, CLASSES * TARGETS)
            lhs = jnp.concatenate(
                [
                    x
                    for member in range(CLASSES)
                    for x in halves(picked, first + member * TARGETS, TARGETS)
                ],
                axis=1,
            )
            rhs = ops_ref[pl.ds(group * CLASSES, CLASSES)]
            rhs = rhs.reshape(CLASSES * 2 * LANES, 2 * LANES)
            product = jnp.dot(lhs, rhs, preferred_element_type=jnp.float32)
            rows = pl.ds(pl.multiple_of(block * TARGETS, TARGETS), TARGETS)
            for half in range(2):
                total[half, rows, :] += product[:, half * LANES : (half + 1) * LANES]
            return carry

        lax.fori_loop(0, slots // CLASSES, multiply, 0)
        rows = pl.ds(pl.multiple_of(block * TARGETS, TARGETS), TARGETS)
        for half in range(2):
            staged[rows, half * LANES : (half + 1) * LANES] = total[half, rows, :]
        send_out(block).start()
        return carry

    lax.fori_loop(0, leaves // TARGETS, block_step, 0)
    for block in range(leaves // TARGETS):
        send_out(block).wait()


def on_device(multipoles, send_rows, send_count, lists, operators, top_local, ancestor, down_ops):
    leaves, coefs = multipoles.shape
    slots = operators.shape[0]
    peers = lax.axis_size("morton")
    me = lax.axis_index("morton")
    tops = 2 * top_local.shape[0]
    pitch = 2 * send_rows.shape[2] + tops
    total_rows = peers * pitch
    vmem = pl.BlockSpec(memory_space=pltpu.VMEM)
    smem = pl.BlockSpec(memory_space=pltpu.SMEM)
    hbm = pl.BlockSpec(memory_space=pltpu.HBM)
    outgoing = pl.pallas_call(
        functools.partial(send_kernel, peers),
        out_shape=jax.ShapeDtypeStruct((peers, pitch, LANES), jnp.bfloat16),
        in_specs=[smem, hbm, hbm, hbm],
        out_specs=hbm,
        scratch_shapes=[
            pltpu.SMEM(send_rows.shape[1:], jnp.int32),
            pltpu.VMEM(multipoles.shape, jnp.bfloat16),
            pltpu.VMEM(top_local.shape, jnp.float32),
            pltpu.VMEM((2 * leaves, LANES), jnp.float32),
            pltpu.VMEM((total_rows, LANES), jnp.float32),
            pltpu.VMEM((peers, pitch, LANES), jnp.bfloat16),
            pltpu.SemaphoreType.DMA((6,)),
            pltpu.SemaphoreType.DMA((peers // PEER_GROUP,)),
        ],
        compiler_params=pltpu.CompilerParams(vmem_limit_bytes=60 * 2**20),
        name="send_rows",
    )(me[None], send_rows, multipoles, top_local)
    incoming = lax.all_to_all(outgoing, "morton", split_axis=0, concat_axis=0, tiled=True)
    ranks = lax.axis_size("coef")
    forward = [(i, i + 1) for i in range(ranks - 1)]
    backward = [(i + 1, i) for i in range(ranks - 1)]
    low = lax.ppermute(multipoles[leaves // 2 :], "coef", forward)
    high = lax.ppermute(multipoles[: leaves // 2], "coef", backward)
    entries = jnp.where(lists >= 0, 2 * lists, BLANK).T
    entries = entries.reshape(slots, leaves // TARGETS, TARGETS).transpose(1, 0, 2).reshape(-1)
    octants = down_ops.shape[0]
    parents = ancestor.reshape(leaves // octants, octants).T
    chunk = SLOT_ROWS
    return pl.pallas_call(
        functools.partial(main_kernel, peers),
        out_shape=jax.ShapeDtypeStruct((leaves, coefs), jnp.float32),
        in_specs=[vmem] * 6 + [hbm] * 2,
        out_specs=hbm,
        scratch_shapes=[
            pltpu.VMEM((BLANK + 16, LANES), jnp.float32),
            pltpu.SMEM((chunk,), jnp.int32),
            pltpu.SMEM((chunk,), jnp.int32),
            pltpu.VMEM((peers * tops, LANES), jnp.float32),
            pltpu.VMEM((2 * TARGETS * slots, LANES), jnp.float32),
            pltpu.VMEM((2, leaves, LANES), jnp.float32),
            pltpu.VMEM(operators.shape, operators.dtype),
            pltpu.VMEM(down_ops.shape, down_ops.dtype),
            pltpu.VMEM((leaves, coefs), jnp.float32),
            pltpu.SemaphoreType.DMA((2,)),
            pltpu.SemaphoreType.DMA((2,)),
            pltpu.SemaphoreType.DMA((leaves // TARGETS,)),
        ],
        compiler_params=pltpu.CompilerParams(vmem_limit_bytes=48 * 2**20),
        name="far_field",
    )(entries, parents, low, multipoles, high, incoming, operators, down_ops)


def solution(mesh):
    placed = (
        P(("morton", "coef"), None),
        P(("morton", "coef"), None, None),
        P(("morton", "coef"), None),
        P(("morton", "coef"), None),
        P(),
        P("morton", None),
        P(("morton", "coef")),
        P(),
    )
    return jax.shard_map(
        on_device,
        mesh=mesh,
        in_specs=placed,
        out_specs=P(("morton", "coef"), None),
        check_vma=False,
    )
```
